32 devices in a mesh: wide: 16 (over z, x, core), narrow: 2 (over y).
Axes of the slice: x: 2, y: 2, z: 4, core: 2. Of those that a mesh axis runs over, the one named last changes fastest.
Arguments:
- resid: bfloat16 [1024, 5120], P('wide'), may hold values from -6 to 6
- final_gain: float32 [5120], replicated, may hold values from 0.25 to 1.75
- unembed: bfloat16 [16384, 5120], P('narrow', 'wide'), may hold values from -12 to 12
- labels: int32 [1024, 4], replicated, may hold values from 0 to 16383
- layer_in: bfloat16 [1024, 5120], P('wide'), may hold values from -6 to 6
- gate_value: bfloat16 [1024, 13824], P('wide', 'narrow'), may hold values from -0.29882812 to 2
- down_weight: bfloat16 [13824, 5120], P('narrow', 'wide'), may hold values from -0.078125 to 0.078125
- basis_in: bfloat16 [5120, 5120], P('wide', 'narrow'), may hold values from -0.078125 to 0.078125
- basis_out: bfloat16 [13824, 13824], P('narrow', 'wide'), may hold values from -0.0546875 to 0.0546875
Outputs:
- corrected: float32 [13824, 5120], P('wide', 'narrow')
The draws below stay inside these ranges and needn't reach their ends.
All inputs are finite; a program needn't handle non-finite values.
Results may differ from the reference program's by a relative error of at most 0.002.
The reference program's roundings to bfloat16 on the way (of `normed`, `probs`, `back`, `gated`, `rotated` and `inputs_rot`) count: a program that leaves them out, or rounds other values in their place, can miss the bound.
Values may be sent and summed in bfloat16 or wider, within the bound.
No kernel may reach another device: no remote copies, remote signals or barrier semaphores. Data moves between devices by JAX's collectives and lax.ppermute only.
A program may use at most 192 MiB of HBM per device.

```python
import math
import jax
import jax.numpy as jnp
from jax import lax

D = 5120
FW = 13824
VOCAB = 16384
SEQ = 256
SAMPLES = 4
EXAMPLES = 4
TOKENS = 1024


def draw_unembed(key, part):
    base = jax.random.normal(key, (VOCAB, D), jnp.float32) * (4.0 / math.sqrt(D))
    return jnp.clip(base, -12.0, 12.0).astype(jnp.bfloat16)


def with_ends(array, key, low, high):
    dims = array.shape
    index_at = [jax.random.randint(jax.random.fold_in(key, axis), (), 0, dims[axis]) for axis in range(len(dims))]
    array = array.at[tuple(index_at)].set(low)
    longest = dims.index(max(dims))
    index_at[longest] = (index_at[longest] + 1) % dims[longest]
    return array.at[tuple(index_at)].set(high)


def steps_of(key, extent, split, least, top_value):
    def one(dim, blocks):
        heights = jax.random.uniform(jax.random.fold_in(jax.random.fold_in(key, 6), dim), (blocks,), jnp.float32, least / len(split), top_value / len(split))
        return jnp.repeat(jnp.exp(heights), extent[dim] // blocks).reshape((-1,) + (1,) * (len(extent) - dim - 1))

    gain = one(*split[0])
    for cut in split[1:]:
        gain = gain * one(*cut)
    return gain


def normal_values(key, extent, deviation, most, split=(), kind=jnp.bfloat16):
    gain = steps_of(key, extent, split, -0.22, 0.18) if split else 1.0
    entries = jax.random.normal(key, extent, jnp.float32) * deviation * gain
    return jnp.minimum(jnp.maximum(entries, -most), most).astype(kind)


def setup_inputs(seed: int = 0) -> dict:
    key_list = jax.random.split(jax.random.key(seed), 10)
    resid = normal_values(key_list[0], (TOKENS, D), 1.0, 6.0, ((0, 16),))
    final_gain = jnp.clip(1.0 + 0.15 * jax.random.normal(key_list[1], (D,), jnp.float32), 0.25, 1.75)
    unembed = draw_unembed(jax.random.fold_in(key_list[9], 71), 0)
    labels = with_ends(jax.random.randint(key_list[3], (TOKENS, SAMPLES), 0, VOCAB), jax.random.fold_in(key_list[3], 1), 0, VOCAB - 1).astype(jnp.int32)
    layer_in = normal_values(key_list[4], (TOKENS, D), 1.0, 6.0, ((0, 16),))
    gate_value = jnp.clip(-0.29882812 + 2.2988281 * jax.random.uniform(key_list[5], (TOKENS, FW), jnp.float32) ** steps_of(key_list[5], (TOKENS, FW), ((0, 16), (1, 2)), -0.2, 0.2), -0.29882812, 2.0).astype(jnp.bfloat16)
    down_weight = normal_values(key_list[6], (FW, D), D ** -0.5, 0.078125, ((0, 2), (1, 16)))
    basis_in = normal_values(key_list[7], (D, D), D ** -0.5, 0.078125, ((0, 16), (1, 2)))
    basis_out = normal_values(key_list[8], (FW, FW), FW ** -0.5, 0.0546875, ((0, 2), (1, 16)))
    return {"resid": resid, "final_gain": final_gain, "unembed": unembed, "labels": labels, "layer_in": layer_in, "gate_value": gate_value, "down_weight": down_weight, "basis_in": basis_in, "basis_out": basis_out}


EPSILON = 1e-05

def reference(resid, final_gain, unembed, labels, layer_in, gate_value, down_weight, basis_in, basis_out):
    resid_float = resid.astype(jnp.float32)
    inverse = lax.rsqrt(lax.optimization_barrier(jnp.mean(resid_float * resid_float, axis=1)) + EPSILON)
    normed = (resid_float * inverse[:, None] * final_gain).astype(jnp.bfloat16)
    logits = lax.dot_general(normed, unembed, (((1,), (1,)), ((), ())), preferred_element_type=jnp.float32)
    largest = lax.optimization_barrier(jnp.max(logits, axis=1, keepdims=True))
    scaled = jnp.exp(logits - largest)
    probs = (scaled / lax.optimization_barrier(jnp.sum(scaled, axis=1, keepdims=True))).astype(jnp.bfloat16)
    common = jnp.dot(probs, unembed, preferred_element_type=jnp.float32)
    picked = jnp.take(unembed, labels.astype(jnp.int32), axis=0).astype(jnp.float32)
    label_grads = common[:, None, :] - picked
    inner = lax.optimization_barrier(jnp.sum(final_gain * label_grads * resid_float[:, None, :], axis=2))
    back = inverse[:, None, None] * final_gain * label_grads - resid_float[:, None, :] * (inverse ** 3)[:, None, None] * inner[:, :, None] / D
    back = back.astype(jnp.bfloat16).reshape(TOKENS * SAMPLES, D)
    hidden_grads = lax.dot_general(back, down_weight, (((1,), (1,)), ((), ())), preferred_element_type=jnp.float32)
    gated = (hidden_grads.reshape(TOKENS, SAMPLES, FW) * gate_value.astype(jnp.float32)[:, None, :]).astype(jnp.bfloat16)
    rotated = jnp.dot(gated.reshape(TOKENS * SAMPLES, FW), basis_out, preferred_element_type=jnp.float32).astype(jnp.bfloat16)
    rotated = rotated.reshape(EXAMPLES, SEQ, SAMPLES, FW)
    inputs_rot = jnp.dot(layer_in, basis_in, preferred_element_type=jnp.float32).astype(jnp.bfloat16).reshape(EXAMPLES, SEQ, D)

    def accumulate(total, pair):
        rot_example, input_example = pair
        for sample in range(SAMPLES):
            block = lax.dot_general(rot_example[:, sample, :], input_example, (((0,), (0,)), ((), ())), preferred_element_type=jnp.float32)
            total = total + block * block
        return (total, None)
    total, _ = lax.scan(accumulate, jnp.zeros((FW, D), jnp.float32), (rotated, inputs_rot))
    return total / (EXAMPLES * SAMPLES)
```

```python
import jax
import jax.numpy as jnp
from jax import lax
from jax.experimental import pallas as pl
from jax.experimental.pallas import tpu as pltpu
from jax.sharding import PartitionSpec as P

SEQ = 256
EPSILON = 1e-05
BF = jnp.bfloat16
F32 = jnp.float32


def dot(left, right, dims):
    return lax.dot_general(left, right, (dims, ((), ())), preferred_element_type=F32)


def after(arrays, first):
    return lax.optimization_barrier((arrays, first))[0]


def shift_pairs(chips, by_line, by_side, by_core):
    lines = chips // 2
    pairs = []
    for line in range(lines):
        for side in range(2):
            for core in range(2):
                there = ((line + by_line) % lines * 2 + (side + by_side) % 2) * 2 + (core + by_core) % 2
                pairs.append(((line * 2 + side) * 2 + core, there))
    return pairs


def swap_core(array):
    wide = lax.axis_size("wide")
    return lax.ppermute(array, "wide", [(i, i ^ 1) for i in range(wide)])


def join_core(array, axis):
    got = swap_core(array)
    core = lax.axis_index("wide") % 2
    return jnp.concatenate(
        [jnp.where(core == 0, array, got), jnp.where(core == 0, got, array)], axis=axis
    )


def swap_narrow(parts):
    if lax.axis_size("narrow") != 2:
        return lax.all_to_all(parts, "narrow", split_axis=0, concat_axis=0, tiled=True)
    me = lax.axis_index("narrow")
    got = lax.ppermute(
        jnp.where(me == 0, parts[1], parts[0]), "narrow", [(0, 1), (1, 0)]
    )
    return jnp.stack([jnp.where(me == 0, parts[0], got), jnp.where(me == 0, got, parts[1])])


def sum_narrow(parts):
    if lax.axis_size("narrow") != 2:
        return lax.psum_scatter(parts, "narrow", scatter_dimension=0, tiled=True)[0]
    me = lax.axis_index("narrow")
    got = lax.ppermute(
        jnp.where(me == 0, parts[1], parts[0]), "narrow", [(0, 1), (1, 0)]
    )
    return jnp.where(me == 0, parts[0], parts[1]) + got


def join_narrow(array, axis):
    if lax.axis_size("narrow") != 2:
        return lax.all_gather(array, "narrow", axis=axis, tiled=True)
    me = lax.axis_index("narrow")
    got = lax.ppermute(array, "narrow", [(0, 1), (1, 0)])
    return jnp.concatenate(
        [jnp.where(me == 0, array, got), jnp.where(me == 0, got, array)], axis=axis
    )


def ring_chip(place, chips):
    lines = chips // 2
    return jnp.where(place < lines, 2 * place, 2 * (chips - 1 - place) + 1)


def ring_gather(block, odd):
    wide = lax.axis_size("wide")
    chips = wide // 2
    lines = chips // 2
    order = [2 * i if i < lines else 2 * (chips - 1 - i) + 1 for i in range(chips)]
    chip = lax.axis_index("wide") // 2
    place = jnp.where(chip % 2 == 0, chip // 2, chips - 1 - chip // 2)
    size = block.shape[0]
    out = jnp.zeros((chips * size,) + block.shape[1:], block.dtype)
    out = lax.dynamic_update_slice_in_dim(out, block, chip * size, 0)
    many = chips // 2
    for step, hops in ((1, chips - 1 - many if odd else many), (-1, many if odd else chips - 1 - many)):
        pairs = [
            (2 * order[i] + core, 2 * order[(i + step) % chips] + core)
            for i in range(chips)
            for core in range(2)
        ]
        held = block
        for hop in range(1, hops + 1):
            held = lax.ppermute(held, "wide", pairs)
            source = ring_chip((place - step * hop) % chips, chips)
            out = lax.dynamic_update_slice_in_dim(out, held, source * size, 0)
    return out


def chip_exchange(array, axis):
    wide = lax.axis_size("wide")
    chips = wide // 2
    chip = lax.axis_index("wide") // 2
    line, side = chip // 2, chip % 2
    size = array.shape[axis] // chips
    shape = list(array.shape)
    shape[axis] = size
    out = jnp.zeros([chips] + shape, array.dtype)
    for by_line in range(chips // 2):
        for by_side in range(2):
            to = (line + by_line) % (chips // 2) * 2 + (side + by_side) % 2
            piece = lax.dynamic_slice_in_dim(array, to * size, size, axis)
            if by_line or by_side:
                piece = lax.ppermute(piece, "wide", shift_pairs(chips, by_line, by_side, 0))
            source = (line - by_line) % (chips // 2) * 2 + (side - by_side) % 2
            out = lax.dynamic_update_slice_in_dim(out, piece[None], source, 0)
    return out


def merge_stats(mine, got):
    largest = jnp.maximum(mine[0], got[0])
    a, b = jnp.exp(mine[0] - largest), jnp.exp(got[0] - largest)
    sums = mine[1:3] * a + got[1:3] * b
    return jnp.concatenate([largest[None], sums, mine[3:] + got[3:]])


def share_stats(stats):
    for axis in ("wide", "narrow"):
        count = lax.axis_size(axis)
        bit = 1
        while bit < count:
            got = lax.ppermute(stats, axis, [(i, i ^ bit) for i in range(count)])
            stats = merge_stats(stats, got)
            bit *= 2
    return stats


def square_kernel(samples, rotated_ref, inputs_ref, total_ref, out_ref):
    seq = inputs_ref.shape[1]
    total = total_ref[...]
    for s in range(samples):
        block = dot(rotated_ref[:, s * seq : (s + 1) * seq], inputs_ref[...], ((1,), (1,)))
        total = total + block * block
    out_ref[...] = total


def add_squares(rotated, inputs, total, samples):
    rows, dirs = rotated.shape[0], inputs.shape[0]
    row_block = 432 if rows % 432 == 0 else rows
    dir_block = 512 if dirs % 512 == 0 else dirs
    spec = pl.BlockSpec((row_block, dir_block), lambda i, j: (i, j))
    return pl.pallas_call(
        lambda *refs: square_kernel(samples, *refs),
        out_shape=jax.ShapeDtypeStruct((rows, dirs), F32),
        grid=(rows // row_block, dirs // dir_block),
        in_specs=[
            pl.BlockSpec((row_block, rotated.shape[1]), lambda i, j: (i, 0)),
            pl.BlockSpec((dir_block, inputs.shape[1]), lambda i, j: (j, 0)),
            spec,
        ],
        out_specs=spec,
        input_output_aliases={2: 0},
        compiler_params=pltpu.CompilerParams(vmem_limit_bytes=32 * 1024 * 1024),
        cost_estimate=pl.CostEstimate(
            flops=2 * rows * dirs * rotated.shape[1],
            bytes_accessed=8 * rows * dirs + 2 * rotated.size + 2 * inputs.size,
            transcendentals=0,
        ),
    )(rotated, inputs, total)


def per_device(
    resid, final_gain, unembed, labels, layer_in, gate_value, down_weight, basis_in, basis_out
):
    wide = lax.axis_size("wide")
    narrow = lax.axis_size("narrow")
    chips = wide // 2
    place = lax.axis_index("wide")
    chip, core = place // 2, place % 2
    narrow_place = lax.axis_index("narrow")
    width = resid.shape[1]
    tokens, samples = labels.shape
    examples = tokens // SEQ
    vocab_part = unembed.shape[0]
    hidden_part = down_weight.shape[0]
    vocab_own = vocab_part // wide
    hidden_own = hidden_part // chips
    chip_cols = width // chips
    step = tokens // (wide * narrow)
    owners = chips // examples
    few = owners * step

    def regroup(array):
        rest = array.shape[1:]
        array = array.reshape((examples, owners, 2, narrow, step) + rest)
        return jnp.transpose(array, (2, 0, 3, 1, 4) + tuple(range(5, 5 + len(rest)))).reshape(
            (tokens,) + rest
        )

    resid_all = regroup(lax.all_gather(resid, "wide", axis=0, tiled=True))
    unembed_own = lax.all_to_all(unembed.T, "wide", split_axis=1, concat_axis=0, tiled=True)
    labels_all = regroup(labels)

    resid_float = resid_all.astype(F32)
    inverse = lax.rsqrt(jnp.mean(resid_float * resid_float, axis=1) + EPSILON)
    normed = (resid_float * inverse[:, None] * final_gain).astype(BF)
    logits = dot(unembed_own, normed, ((0,), (1,)))
    first_own = narrow_place * vocab_part + place * vocab_own
    entry = lax.broadcasted_iota(jnp.int32, logits.shape, 0) + first_own
    own_max = jnp.max(logits, axis=0)
    own_exp = jnp.exp(logits - own_max)
    stats = [own_max, jnp.sum(own_exp, axis=0), jnp.sum(own_exp * logits, axis=0)]
    for s in range(samples):
        stats.append(jnp.sum(jnp.where(entry == labels_all[:, s], logits, 0.0), axis=0))
    stats = share_stats(jnp.stack(stats))
    probs = (jnp.exp(logits - stats[0]) / stats[1]).astype(BF)
    inner = stats[2] / stats[1] - stats[3:]
    shrink = inner * (inverse * inverse / width)

    unembed_chip = join_core(unembed.T, 0)
    basis_chip = join_core(basis_out.T, 0)

    probs = probs.reshape(vocab_own, 2, tokens // 2)
    keep = jnp.where(core == 0, probs[:, 0], probs[:, 1])
    give = swap_core(jnp.where(core == 0, probs[:, 1], probs[:, 0]))
    probs = jnp.concatenate(
        [jnp.where(core == 0, keep, give), jnp.where(core == 0, give, keep)], axis=0
    )

    def own(array):
        array = array.reshape((2, examples, narrow, few) + array.shape[1:])
        array = lax.dynamic_index_in_dim(array, core, 0, keepdims=False)
        return lax.dynamic_index_in_dim(array, narrow_place, 1, keepdims=False)

    order = lax.dynamic_index_in_dim(
        labels_all.reshape(2, examples, narrow, few, samples), core, 0, keepdims=False
    )
    order = jnp.transpose(order, (1, 0, 3, 2)).reshape(-1)
    shifted = order - narrow_place * vocab_part
    inside = (shifted >= 0) & (shifted < vocab_part)
    picked = jnp.take(unembed_chip.T, jnp.clip(shifted, 0, vocab_part - 1), axis=0)
    picked = jnp.where(inside[:, None], picked, jnp.zeros_like(picked))
    picked = sum_narrow(picked.reshape(narrow, examples, samples * few, chip_cols))

    resid_cols = lax.dynamic_slice_in_dim(own(resid_all), chip * chip_cols, chip_cols, 2)
    inverse_own = own(inverse)
    shrink_own = own(shrink.T)
    gain_cols = lax.dynamic_slice_in_dim(final_gain, chip * chip_cols, chip_cols, 0)

    down_late = after(down_weight, logits)
    down_own = chip_exchange(down_late.T, 1)
    down_own = join_narrow(down_own, 2)
    down_own = join_core(down_own[:, None], 1).reshape(width, narrow * hidden_own)
    gate_late = after(gate_value, logits)
    gates = chip_exchange(gate_late.T, 0)
    gates = gates.reshape(examples, owners, hidden_own, narrow, step)
    gates = swap_narrow(jnp.transpose(gates, (3, 2, 0, 1, 4)))
    gates = gates.reshape(narrow * hidden_own, examples, 1, few)

    layer_late, basis_late = after((layer_in, basis_in), stats)
    layer_all = lax.all_gather(layer_late, "wide", axis=0, tiled=True)
    basis_own = lax.all_to_all(basis_late, "wide", split_axis=1, concat_axis=0, tiled=True)
    inputs_own = dot(basis_own, layer_all, ((0,), (1,))).astype(BF)
    dirs_own = inputs_own.shape[0]
    inputs_own = inputs_own.reshape(dirs_own, examples, owners, 2, narrow, step)
    inputs_own = jnp.transpose(inputs_own, (0, 1, 3, 4, 2, 5)).reshape(dirs_own, tokens)
    inputs_rot = lax.all_gather(inputs_own, "wide", axis=0, tiled=True)

    out_part = basis_out.shape[1]
    corrected = jnp.zeros((out_part, inputs_rot.shape[0]), F32)
    for e in range(examples):
        span = few * narrow
        probs_e = ring_gather(probs[:, e * span : (e + 1) * span], e % 2)
        common = dot(unembed_chip, probs_e, ((1,), (0,)))
        common = sum_narrow(jnp.transpose(common.reshape(chip_cols, narrow, few), (1, 0, 2)))
        grads = common[:, None] - jnp.transpose(
            picked[e].reshape(samples, few, chip_cols), (2, 0, 1)
        ).astype(F32)
        back = inverse_own[e] * gain_cols[:, None, None] * grads
        back = back - resid_cols[e].T.astype(F32)[:, None] * shrink_own[e].T
        back = back.astype(BF).reshape(chip_cols, samples * few)
        back = ring_gather(back, e % 2)
        hidden = dot(down_own, back, ((0,), (0,))).reshape(narrow * hidden_own, samples, few)
        gated = (hidden * gates[:, e].astype(F32)).astype(BF)
        gated = swap_narrow(gated.reshape(narrow, hidden_own, samples, few))
        gated = jnp.transpose(gated, (1, 2, 0, 3)).reshape(hidden_own, samples * span)
        gated = ring_gather(gated, e % 2)
        rotated = dot(basis_chip, gated, ((1,), (0,)))
        rotated = rotated.reshape(2 * out_part, narrow, samples * span // narrow)
        rotated = sum_narrow(jnp.transpose(rotated, (1, 0, 2))).astype(BF)
        rotated = rotated.reshape(2, out_part, samples * span // narrow)
        keep = jnp.where(core == 0, rotated[0], rotated[1])
        give = swap_core(jnp.where(core == 0, rotated[1], rotated[0]))
        rotated = jnp.stack(
            [jnp.where(core == 0, keep, give), jnp.where(core == 0, give, keep)], axis=1
        )
        rotated = join_narrow(rotated, 2).reshape(out_part, 2, samples, span)
        rotated = jnp.transpose(rotated, (0, 2, 1, 3)).reshape(out_part, samples * SEQ)
        corrected = add_squares(
            rotated, inputs_rot[:, e * SEQ : (e + 1) * SEQ], corrected, samples
        )
    return corrected / (examples * samples)


def solution(mesh):
    in_specs = (
        P("wide", None),
        P(),
        P("narrow", "wide"),
        P(),
        P("wide", None),
        P("wide", "narrow"),
        P("narrow", "wide"),
        P("wide", "narrow"),
        P("narrow", "wide"),
    )
    out_specs = P("wide", "narrow")
    return jax.shard_map(
        per_device, mesh=mesh, in_specs=in_specs, out_specs=out_specs, check_vma=False
    )
```

```python
import jax
import jax.numpy as jnp
from jax import lax
from jax.experimental import pallas as pl
from jax.experimental.layout import Layout, with_layout_constraint
from jax.experimental.pallas import tpu as pltpu
from jax.sharding import PartitionSpec as P

SEQ = 256
EPSILON = 1e-05
BF = jnp.bfloat16
F32 = jnp.float32


def dot(left, right, dims):
    return lax.dot_general(left, right, (dims, ((), ())), preferred_element_type=F32)


def zero_after(array):
    first = lax.slice(array, (0,) * array.ndim, (1,) * array.ndim).reshape(())
    return jnp.minimum(jnp.abs(first.astype(F32)), 0.0)


def swap_core(array):
    wide = lax.axis_size("wide")
    return lax.ppermute(array, "wide", [(i, i ^ 1) for i in range(wide)])


def by_core(own, other):
    core = lax.axis_index("wide") % 2
    return jnp.where(core == 0, own, other), jnp.where(core == 0, other, own)


def plain(array):
    return with_layout_constraint(array, Layout(tuple(range(array.ndim))))


def join_core(array, other):
    core = lax.axis_index("wide") % 2
    out = plain(jnp.zeros((array.shape[0], 2) + array.shape[1:], array.dtype))
    out = lax.dynamic_update_slice_in_dim(out, array[:, None], core, 1)
    out = lax.dynamic_update_slice_in_dim(out, other[:, None], 1 - core, 1)
    return plain(out)


def swap_narrow(parts):
    if lax.axis_size("narrow") != 2:
        got = lax.all_to_all(jnp.stack(parts), "narrow", split_axis=0, concat_axis=0, tiled=True)
        return [got[n] for n in range(len(parts))]
    me = lax.axis_index("narrow")
    got = lax.ppermute(jnp.where(me == 0, parts[1], parts[0]), "narrow", [(0, 1), (1, 0)])
    return [jnp.where(me == 0, parts[0], got), jnp.where(me == 0, got, parts[1])]


def sum_narrow(parts):
    if lax.axis_size("narrow") != 2:
        return lax.psum_scatter(jnp.stack(parts), "narrow", scatter_dimension=0, tiled=True)[0]
    me = lax.axis_index("narrow")
    got = lax.ppermute(jnp.where(me == 0, parts[1], parts[0]), "narrow", [(0, 1), (1, 0)])
    return jnp.where(me == 0, parts[0], parts[1]) + got


def cut(array, count, axis):
    size = array.shape[axis] // count
    return [lax.slice_in_dim(array, n * size, (n + 1) * size, axis=axis) for n in range(count)]


def ring_chip(place, chips):
    lines = chips // 2
    return jnp.where(place < lines, 2 * place, 2 * (chips - 1 - place) + 1)


def ring_gather(block, odd):
    wide = lax.axis_size("wide")
    chips = wide // 2
    lines = chips // 2
    order = [2 * i if i < lines else 2 * (chips - 1 - i) + 1 for i in range(chips)]
    chip = lax.axis_index("wide") // 2
    place = jnp.where(chip % 2 == 0, chip // 2, chips - 1 - chip // 2)
    out = plain(jnp.zeros((chips,) + block.shape, block.dtype))
    out = lax.dynamic_update_slice_in_dim(out, block[None], chip, 0)
    many = chips // 2
    mark = last = block
    for step, hops in ((1, chips - 1 - many if odd else many), (-1, many if odd else chips - 1 - many)):
        pairs = [
            (2 * order[i] + core, 2 * order[(i + step) % chips] + core)
            for i in range(chips)
            for core in range(2)
        ]
        held = block
        for hop in range(1, hops + 1):
            held = lax.ppermute(held, "wide", pairs)
            source = ring_chip((place - step * hop) % chips, chips)
            out = lax.dynamic_update_slice_in_dim(out, held[None], source, 0)
            if hop == 2:
                mark = held
            last = held
    return plain(out), mark, last


def chip_exchange(array, axis, start):
    wide = lax.axis_size("wide")
    chips = wide // 2
    lines = chips // 2
    chip = lax.axis_index("wide") // 2
    line, side = chip // 2, chip % 2
    size = array.shape[axis] // chips
    shape = list(array.shape)
    shape[axis] = size
    out = plain(jnp.zeros([chips] + shape, array.dtype))
    for by_line in range(lines):
        for by_side in range(2):
            to = (line + by_line) % lines * 2 + (side + by_side) % 2
            piece = lax.dynamic_slice_in_dim(array, to * size + start, size, axis)
            if by_line or by_side:
                pairs = [
                    (2 * q + core, 2 * ((q // 2 + by_line) % lines * 2 + (q % 2 + by_side) % 2) + core)
                    for q in range(chips)
                    for core in range(2)
                ]
                piece = lax.ppermute(piece, "wide", pairs)
            source = (line - by_line) % lines * 2 + (side - by_side) % 2
            out = lax.dynamic_update_slice_in_dim(out, piece[None], source, 0)
    return plain(out)


def merge_stats(mine, got):
    largest = jnp.maximum(mine[0], got[0])
    a, b = jnp.exp(mine[0] - largest), jnp.exp(got[0] - largest)
    sums = mine[1:3] * a + got[1:3] * b
    return jnp.concatenate([largest[None], sums, mine[3:] + got[3:]])


def share_stats(stats):
    for axis in ("wide", "narrow"):
        count = lax.axis_size(axis)
        bit = 1
        while bit < count:
            got = lax.ppermute(stats, axis, [(i, i ^ bit) for i in range(count)])
            stats = merge_stats(stats, got)
            bit *= 2
    return stats


def square_kernel(samples, scale, first, inputs_ref, *refs):
    parts, out_ref = refs[:-1], refs[-1]
    total = 0.0
    if not first:
        total, parts = parts[0][...], parts[1:]
    for s in range(samples):
        pieces = []
        for part in parts:
            size = part.shape[1] // samples
            pieces.append(part[:, s * size : (s + 1) * size])
        left = jnp.concatenate(pieces, axis=1) if len(pieces) > 1 else pieces[0]
        block = dot(left, inputs_ref[...], ((1,), (1,)))
        total = total + block * block
    out_ref[...] = total if scale is None else total * scale


def add_squares(parts, inputs, total, samples, scale):
    rows, dirs = parts[0].shape[0], inputs.shape[0]
    row_block = 432 if rows % 432 == 0 else rows
    dir_block = 512 if dirs % 512 == 0 else dirs
    spec = pl.BlockSpec((row_block, dir_block), lambda i, j: (i, j))
    size = sum(part.shape[1] for part in parts)
    return pl.pallas_call(
        lambda *refs: square_kernel(samples, scale, total is None, *refs),
        out_shape=jax.ShapeDtypeStruct((rows, dirs), F32),
        grid=(rows // row_block, dirs // dir_block),
        in_specs=[pl.BlockSpec((dir_block, inputs.shape[1]), lambda i, j: (j, 0))]
        + ([] if total is None else [spec])
        + [pl.BlockSpec((row_block, part.shape[1]), lambda i, j: (i, 0)) for part in parts],
        out_specs=spec,
        input_output_aliases={1: 0} if total is not None and scale is None else {},
        compiler_params=pltpu.CompilerParams(vmem_limit_bytes=32 * 1024 * 1024),
        cost_estimate=pl.CostEstimate(
            flops=2 * rows * dirs * size,
            bytes_accessed=8 * rows * dirs + 2 * rows * size + 2 * inputs.size,
            transcendentals=0,
        ),
    )(inputs, *([] if total is None else [total]), *parts)


def per_device(
    resid, final_gain, unembed, labels, layer_in, gate_value, down_weight, basis_in, basis_out
):
    wide = lax.axis_size("wide")
    narrow = lax.axis_size("narrow")
    chips = wide // 2
    place = lax.axis_index("wide")
    chip, core = place // 2, place % 2
    narrow_place = lax.axis_index("narrow")
    own_tokens, width = resid.shape
    tokens, samples = labels.shape
    examples = tokens // SEQ
    cols = width // wide
    chip_cols = width // chips
    vocab_part = unembed.shape[0]
    vocab_own = vocab_part // wide
    hidden_part = down_weight.shape[0]
    hidden_own = hidden_part // chips
    half = SEQ // 2
    few = half // narrow
    group = 2 if examples % 2 == 0 else 1

    share = own_tokens // narrow
    mine = lax.dynamic_slice_in_dim(
        jnp.stack([resid, layer_in]), narrow_place * share, share, 1
    )
    ring, _, last = ring_gather(mine, 0)

    def all_tokens(part):
        rest = part.shape[2:]
        if narrow == 2:
            other = lax.ppermute(part, "narrow", [(0, 1), (1, 0)])
            out = plain(jnp.zeros((chips, 2) + part.shape[1:], part.dtype))
            out = lax.dynamic_update_slice_in_dim(out, part[:, None], narrow_place, 1)
            out = lax.dynamic_update_slice_in_dim(out, other[:, None], 1 - narrow_place, 1)
        else:
            out = lax.all_gather(part, "narrow", axis=1)
        out = out.reshape((chips, own_tokens) + rest)
        return join_core(out, swap_core(out)).reshape((tokens,) + rest)

    resid_all = all_tokens(ring[:, 0])
    layer_all = all_tokens(ring[:, 1] + zero_after(resid_all).astype(BF))

    unembed_own = lax.all_to_all(
        unembed.T + zero_after(last).astype(BF), "wide", split_axis=1, concat_axis=0, tiled=True
    )

    unembed_other = swap_core(unembed.T)
    basis_other = swap_core(basis_out.T)

    def own(array):
        array = array.reshape((examples, 2, narrow, few) + array.shape[1:])
        array = lax.dynamic_index_in_dim(array, core, 1, keepdims=False)
        return lax.dynamic_index_in_dim(array, narrow_place, 1, keepdims=False)

    def chip_columns(array):
        return jnp.concatenate(
            [
                lax.dynamic_slice_in_dim(array, (2 * chip + which) * cols, cols, array.ndim - 1)
                for which in (core, 1 - core)
            ],
            axis=-1,
        )

    order = lax.dynamic_index_in_dim(
        labels.reshape(examples, 2, narrow, few, samples), core, 1, keepdims=False
    )
    order = jnp.transpose(order, (1, 0, 3, 2)).reshape(-1)
    shifted = order - narrow_place * vocab_part
    inside = (shifted >= 0) & (shifted < vocab_part)
    shifted = jnp.clip(shifted, 0, vocab_part - 1)
    picked = [jnp.take(part, shifted, axis=0) for part in (unembed, unembed_other.T)]
    picked = jnp.concatenate(picked, axis=1)
    picked = jnp.where(inside[:, None], picked, jnp.zeros_like(picked))
    picked = sum_narrow(cut(picked, narrow, 0)).reshape(examples, samples, few, chip_cols)
    picked = jnp.transpose(picked, (0, 3, 1, 2))

    both = jnp.concatenate([down_weight.T, gate_value], axis=0)
    both = chip_exchange(both, 1, zero_after(unembed_own).astype(jnp.int32))
    down_own, gates = both[:, :cols], both[:, cols:]
    gates = join_core(gates, swap_core(gates))
    gates = gates.reshape(examples, 2, narrow, few, hidden_own)
    gates = lax.dynamic_index_in_dim(gates, core, 1, keepdims=False)
    gates = swap_narrow([jnp.transpose(gates[:, n], (0, 2, 1)) for n in range(narrow)])
    gates = jnp.concatenate(gates, axis=1)[:, :, None]

    basis_own = lax.all_to_all(
        basis_in + zero_after(both).astype(BF), "wide", split_axis=1, concat_axis=0, tiled=True
    )

    resid_float = resid_all.astype(F32)
    inverse = lax.rsqrt(jnp.mean(resid_float * resid_float, axis=1) + EPSILON)
    for array in (picked, basis_other, layer_all, basis_own, gates):
        inverse = inverse + zero_after(array)
    normed = (resid_float * inverse[:, None] * final_gain).astype(BF)
    logits = dot(unembed_own, normed, ((0,), (1,)))
    first_own = narrow_place * vocab_part + place * vocab_own
    entry = lax.broadcasted_iota(jnp.int32, logits.shape, 0) + first_own
    own_max = jnp.max(logits, axis=0)
    own_exp = jnp.exp(logits - own_max)
    stats = [own_max, jnp.sum(own_exp, axis=0), jnp.sum(own_exp * logits, axis=0)]
    for s in range(samples):
        stats.append(jnp.sum(jnp.where(entry == labels[:, s], logits, 0.0), axis=0))
    stats = share_stats(jnp.stack(stats))
    probs = (jnp.exp(logits - stats[0]) / stats[1]).astype(BF)
    inner = stats[2] / stats[1] - stats[3:]
    shrink = inner * (inverse * inverse / width)
    late = zero_after(stats)
    down_own = down_own + (zero_after(gates) + late).astype(BF)
    if narrow == 2:
        down_other = lax.ppermute(down_own, "narrow", [(0, 1), (1, 0)])

    probs = probs.reshape(vocab_own, examples, 2, half)
    keep = jnp.where(core == 0, probs[:, :, 0], probs[:, :, 1]).reshape(vocab_own, tokens // 2)
    give = jnp.where(core == 0, probs[:, :, 1], probs[:, :, 0]).reshape(vocab_own, tokens // 2)
    probs = jnp.concatenate(by_core(keep, swap_core(give)), axis=0)

    resid_cols = jnp.transpose(chip_columns(own(resid_all)), (0, 2, 1))
    inverse_own = own(inverse)
    shrink_own = jnp.transpose(own(shrink.T), (0, 2, 1))
    gain_cols = chip_columns(final_gain)

    inputs_own = (dot(basis_own, layer_all, ((0,), (1,))) + late).astype(BF)
    inputs_rot, _, _ = ring_gather(inputs_own, 1)
    inputs_rot = join_core(inputs_rot, swap_core(inputs_rot)).reshape(-1, tokens)
    dirs = inputs_rot.shape[0]

    def inputs_of(e):
        one = inputs_rot[:, e * SEQ : (e + 1) * SEQ]
        if narrow != 2:
            return one
        own_core, other_core = by_core(one[:, :half], one[:, half:])
        pieces = [cut(part, 2, 1) for part in (own_core, other_core)]
        mine = [jnp.where(narrow_place == 0, a, b) for a, b in pieces]
        rest = [jnp.where(narrow_place == 0, b, a) for a, b in pieces]
        return jnp.concatenate(mine + rest, axis=1)

    out_part = basis_out.shape[1]
    total = None
    backs = []
    start = jnp.float32(0)
    for g in range(examples // group):
        span = group * half
        probs_g = probs[:, g * span : (g + 1) * span] + start.astype(BF)
        probs_g, mark, _ = ring_gather(probs_g, g % 2)
        start = zero_after(mark)
        probs_g = probs_g.reshape(vocab_part, span)
        common = jnp.concatenate(
            [dot(part, probs_g, ((1,), (0,))) for part in (unembed.T, unembed_other)], axis=0
        )
        common = common.reshape(chip_cols, group, narrow, few)
        common = sum_narrow([common[:, :, n].reshape(chip_cols, group * few) for n in range(narrow)])
        back = []
        for i in range(group):
            e = g * group + i
            grads = common[:, None, i * few : (i + 1) * few] - picked[e].astype(F32)
            one = inverse_own[e] * gain_cols[:, None, None] * grads
            one = one - resid_cols[e].astype(F32)[:, None] * shrink_own[e]
            back.append(one.astype(BF).reshape(chip_cols, samples * few))
        back, _, _ = ring_gather(jnp.concatenate(back, axis=1), g % 2)
        backs += cut(back.reshape(width, -1), group, 1)
    if narrow == 2:
        down_other = down_other + start.astype(BF)
        down_own = jnp.concatenate(
            [
                jnp.where(narrow_place == 0, down_own, down_other),
                jnp.where(narrow_place == 0, down_other, down_own),
            ],
            axis=2,
        )
    else:
        down_own = lax.all_gather(down_own, "narrow", axis=2, tiled=True)
    down_own = jnp.stack([down_own, swap_core(down_own)], axis=1)
    down_own = down_own.reshape(width, narrow * hidden_own)

    starts = [jnp.float32(0)] * (examples + 2)
    ready = jnp.float32(0)
    for e in range(examples):
        hidden = dot(down_own, backs[e], ((0,), (0,)))
        hidden = hidden.reshape(narrow * hidden_own, samples, few)
        gated = (hidden * gates[e].astype(F32) + starts[e]).astype(BF)
        gated = gated.reshape(narrow * hidden_own, samples * few)
        gated = jnp.concatenate(swap_narrow(cut(gated, narrow, 0)), axis=1)
        gated, mark, _ = ring_gather(gated, e % 2)
        starts[e + 1] += zero_after(mark)
        gated = gated.reshape(hidden_part, narrow * samples * few)
        rotated = jnp.stack(
            [dot(part, gated, ((1,), (0,))) + ready for part in (basis_out.T, basis_other)]
        )
        ready = ready if total is None else zero_after(total)
        starts[e + 2] += zero_after(rotated)
        rotated = sum_narrow(cut(rotated, narrow, 2)).astype(BF)
        keep, got = rotated[0], swap_core(rotated[1])
        if narrow == 2:
            across = lax.ppermute(jnp.stack([keep, got]), "narrow", [(0, 1), (1, 0)])
            parts = [keep, got, across[0], across[1]]
        else:
            parts = jnp.stack(by_core(keep, got))
            parts = lax.all_gather(parts, "narrow", axis=0)
            parts = parts.reshape(narrow, 2, out_part, samples, few)
            parts = [jnp.transpose(parts, (2, 3, 1, 0, 4)).reshape(out_part, samples * SEQ)]
        scale = 1.0 / (examples * samples) if e == examples - 1 else None
        total = add_squares(parts, inputs_of(e), total, samples, scale)
    return total


def solution(mesh):
    in_specs = (
        P("wide", None),
        P(),
        P("narrow", "wide"),
        P(),
        P("wide", None),
        P("wide", "narrow"),
        P("narrow", "wide"),
        P("wide", "narrow"),
        P("narrow", "wide"),
    )
    out_specs = P("wide", "narrow")
    return jax.shard_map(
        per_device, mesh=mesh, in_specs=in_specs, out_specs=out_specs, check_vma=False
    )
```
